32 devices in a mesh: dp: 16 (over z, y, core), seq: 2 (over x).
Axes of the slice: x: 2, y: 2, z: 4, core: 2. Of those that a mesh axis runs over, the one named last changes fastest.
Arguments:
- checkpoint: bfloat16 [16384, 8192], P(('dp', 'seq')), may hold values from -6 to 6
- norm_gain: float32 [8192], replicated, may hold values from 0.1 to 1.9
- key_cotangent: bfloat16 [16384, 1024], P(('dp', 'seq')), may hold values from -6 to 6
- positions: int32 [16384], P(('dp', 'seq')), may hold values from 0 to 4095, as said below
- kept_cols: int32 [128, 6], replicated, may hold values from 0 to 15, as said below
- kept_count: int32 [128], replicated, may hold values from 2 to 6
- key_blocks: bfloat16 [128, 6, 4096], P('dp'), may hold values from -0.375 to 0.375
Outputs:
- input_grad: bfloat16 [16384, 8192], P(('dp', 'seq'))
- block_grad: float32 [128, 6, 4096], P('dp', None, 'seq')
The draws below stay inside these ranges and needn't reach their ends.
Inputs may be any that keep to these rules, and one draw needn't show every extreme that they name: `kept_cols`: the 6 entries of a row are different block columns; only the first kept_count entries of a row name kept blocks, the others are unused slots. Inside a document the positions rise by one from token to token.
All inputs are finite; a program needn't handle non-finite values.
Results may differ from the reference program's by a relative error of at most 0.0049.
Values may be sent and summed in bfloat16 or wider, within the bound.
A program may use at most 128 MiB of HBM per device.

```python
import jax
import jax.numpy as jnp
from jax import lax

D = 8192
KVW = 1024
HEAD_DIM = 128
BLK = 64
MOSTR = 6
SEQ_LEN = 1024
TOKENS = 16384
ROW_BLOCKS = 128


def draw_positions(key, part):
    key = jax.random.fold_in(key, 101)
    first_key, second_key = jax.random.split(key)
    index = jnp.arange(TOKENS, dtype=jnp.int32)
    inside = index % SEQ_LEN
    seq_ids = index // SEQ_LEN
    begins = (jax.random.randint(first_key, (TOKENS,), 0, 400) == 0) & (seq_ids != 0) | (inside == 0)
    last = lax.cummax(jnp.where(begins, index, 0), axis=0)
    seqs = TOKENS // SEQ_LEN
    offset = jax.random.randint(second_key, (seqs,), 0, 4096 - SEQ_LEN + 1)
    seq_index = jnp.arange(seqs, dtype=jnp.int32)
    offset = jnp.where(seq_index == 0, 4096 - SEQ_LEN, offset)
    offset = jnp.where(seq_index == 1, 0, offset)
    carried = jnp.repeat(offset, SEQ_LEN)
    first_doc = last % SEQ_LEN == 0
    return (index - last + jnp.where(first_doc, carried, 0)).astype(jnp.int32)


def draw_kept_cols(key, part):
    key = jax.random.fold_in(key, 202)
    rows = D // BLK
    cols = KVW // BLK
    scores = jax.random.randint(key, (rows, cols), 0, 1 << 20) * cols + jnp.arange(cols, dtype=jnp.int32)[None, :]
    order = jnp.argsort(scores, axis=1)
    return order[:, :MOSTR].astype(jnp.int32)


def draw_kept_count(key, part):
    key = jax.random.fold_in(key, 303)
    rows = D // BLK
    first_key, second_key = jax.random.split(key)
    counts = jax.random.randint(first_key, (rows,), 2, MOSTR + 1)
    full = jax.random.randint(second_key, (), 0, rows)
    index = jnp.arange(rows, dtype=jnp.int32)
    counts = jnp.where(index == full, MOSTR, counts)
    counts = jnp.where(index == (full + rows // 2) % rows, 2, counts)
    return counts.astype(jnp.int32)


def levels(rng, dims, cuts, low, top_value):
    def one(dim, shards_of):
        heights = jax.random.uniform(jax.random.fold_in(jax.random.fold_in(rng, 6), dim), (shards_of,), jnp.float32, low / len(cuts), top_value / len(cuts))
        return jnp.repeat(jnp.exp(heights), dims[dim] // shards_of).reshape((-1,) + (1,) * (len(dims) - dim - 1))

    factor_of = one(*cuts[0])
    for cut in cuts[1:]:
        factor_of = factor_of * one(*cut)
    return factor_of


def bell_draw(own_key, extent, scale, limit, cuts=(), kind=jnp.bfloat16):
    entries = scale * jax.random.normal(own_key, extent, jnp.float32)
    if cuts:
        entries = entries * levels(own_key, extent, cuts, -0.22, 0.18)
    return jnp.clip(entries, -limit, limit).astype(kind)


def setup_inputs(seed: int = 0) -> dict:
    keys = jax.random.split(jax.random.key(seed), 8)
    checkpoint = bell_draw(keys[0], (TOKENS, D), 1.0, 6.0, ((0, 32),))
    norm_gain = jnp.clip(1.0 + 0.18 * jax.random.normal(keys[1], (D,), jnp.float32), 0.1, 1.9)
    key_cotangent = bell_draw(keys[2], (TOKENS, KVW), 1.0, 6.0, ((0, 32),))
    positions = draw_positions(jax.random.fold_in(keys[7], 71), 0)
    kept_cols = draw_kept_cols(jax.random.fold_in(keys[7], 71), 0)
    kept_count = draw_kept_count(jax.random.fold_in(keys[7], 71), 0)
    key_blocks = bell_draw(keys[6], (ROW_BLOCKS, MOSTR, BLK * BLK), (4 * BLK) ** -0.5, 0.375, ((0, 16),))
    return dict(checkpoint=checkpoint, norm_gain=norm_gain, key_cotangent=key_cotangent, positions=positions, kept_cols=kept_cols, kept_count=kept_count, key_blocks=key_blocks)


def rope_back(grad, positions):
    heads = KVW // HEAD_DIM
    half = HEAD_DIM // 2
    values = grad.astype(jnp.float32).reshape(-1, heads, 2, half)
    freqs = 10000.0 ** (-2.0 * jnp.arange(half).astype(jnp.float32) / HEAD_DIM)
    angle = positions.astype(jnp.float32)[:, None] * freqs[None, :]
    cosine = jnp.cos(angle)[:, None, :]
    sine = jnp.sin(angle)[:, None, :]
    first = values[:, :, 0] * cosine + values[:, :, 1] * sine
    second = values[:, :, 1] * cosine - values[:, :, 0] * sine
    return jnp.stack([first, second], axis=2).reshape(-1, KVW).astype(jnp.bfloat16)

def densify(blocks, cols, count, rows):
    count_rows = blocks.shape[0]
    col_blocks = KVW // BLK
    live = jnp.arange(MOSTR)[None, :] < count[:, None]
    onehot = ((cols[:, :, None] == jnp.arange(col_blocks)[None, None, :]) & live[:, :, None]).astype(jnp.float32)
    shaped = blocks.astype(jnp.float32).reshape(count_rows, MOSTR, rows, BLK)
    dense = jnp.einsum('nkc,nkij->nicj', onehot, shaped)
    return dense.reshape(count_rows * rows, KVW).astype(jnp.bfloat16)

def reference(checkpoint, norm_gain, key_cotangent, positions, kept_cols, kept_count, key_blocks):
    weight = densify(key_blocks, kept_cols, kept_count, BLK)
    seqs = TOKENS // SEQ_LEN

    def one_sequence(total, pieces):
        rows, cots, pos = pieces
        xf = rows.astype(jnp.float32)
        inv_rms = lax.rsqrt(lax.optimization_barrier(jnp.mean(xf * xf, axis=1, keepdims=True)) + 1e-05)
        normed = (xf * inv_rms * norm_gain).astype(jnp.bfloat16)
        grad_pre = rope_back(cots, pos)
        normed_grad = jnp.dot(grad_pre, weight.T, preferred_element_type=jnp.float32)
        scaled = norm_gain * normed_grad
        grads = inv_rms * scaled - inv_rms ** 3 * xf * lax.optimization_barrier(jnp.mean(scaled * xf, axis=1, keepdims=True))
        total = total + jnp.dot(normed.T, grad_pre, preferred_element_type=jnp.float32)
        return (total, grads.astype(jnp.bfloat16))
    init = jnp.zeros((D, KVW), jnp.float32)
    sums, grads = lax.scan(one_sequence, init, (checkpoint.reshape(seqs, SEQ_LEN, D), key_cotangent.reshape(seqs, SEQ_LEN, KVW), positions.reshape(seqs, SEQ_LEN)))
    input_grad = grads.reshape(TOKENS, D)
    row_blocks = D // BLK
    col_blocks = KVW // BLK
    shaped = sums.reshape(row_blocks, BLK, col_blocks, BLK).transpose(0, 2, 1, 3).reshape(row_blocks, col_blocks, BLK * BLK)
    picked = jnp.take_along_axis(shaped, kept_cols[:, :, None], axis=1)
    live = jnp.arange(MOSTR)[None, :] < kept_count[:, None]
    block_grad = jnp.where(live[:, :, None], picked / jnp.sqrt(jnp.float32(TOKENS)), jnp.float32(0.0))
    return (input_grad, block_grad)
```

```python
import functools
import math

import jax
import jax.numpy as jnp
from jax import lax
from jax.experimental import pallas as pl
from jax.experimental.pallas import tpu as pltpu
from jax.sharding import PartitionSpec as P

D = 8192
KVW = 1024
HEAD_DIM = 128
BLK = 64
MOSTR = 6
SEQ_LEN = 1024
STREAMS = MOSTR // 2
LANES = 128
VMEM = 58 * 1024 * 1024


def bits_of(n):
    return int(math.log2(n))


def stage_plan(dp, seq):
    low = ("dp", 0)
    high = [("dp", b) for b in range(1, bits_of(dp))]
    seqs = [("seq", b) for b in range(bits_of(seq))]
    if dp == 16 and seq == 2:
        y, z1, z2 = high
        (x,) = seqs
        return [[low, x, y, z1, z2], [low, y, x, z1, z2], [low, z1, z2, x, y]]
    return [[low] + seqs + high, [low] + high + seqs, [low] + high[::-1] + seqs]


def bit(value, b):
    return (value // (1 << b)) % 2


def slot_of(order, dp_index, seq_index):
    place = 0
    for axis, b in order[1:]:
        place = place * 2 + bit(dp_index if axis == "dp" else seq_index, b)
    return place


def sums_kernel(dp, seq, x_ref, gain_ref, cot_ref, cos_ref, sin_ref, cols_ref,
                pre_ref, inv_ref, fin_ref,
                sums, first, acc, later, recv_first, recv_later, send_sem, recv_sem):
    tokens = x_ref.shape[0]
    rows_dp = (D // BLK) // dp
    part = BLK // seq
    tile = rows_dp * BLK
    plan = stage_plan(dp, seq)
    stages = len(plan[0])
    me_dp = lax.axis_index("dp")
    me_seq = lax.axis_index("seq")

    def partner(axis, b):
        mine = me_dp if axis == "dp" else me_seq
        other = mine + (1 << b) - 2 * (1 << b) * bit(mine, b)
        return (other, me_seq) if axis == "dp" else (me_dp, other)

    def mybit(axis, b):
        return bit(me_dp if axis == "dp" else me_seq, b)

    barrier = pltpu.get_barrier_semaphore()
    for axis, b in plan[0]:
        pl.semaphore_signal(barrier, inc=1, device_id=partner(axis, b),
                            device_id_type=pl.DeviceIdType.MESH)
    pl.semaphore_wait(barrier, stages)

    tt = 64

    @pl.loop(0, tokens // tt)
    def _(t):
        rows = pl.ds(pl.multiple_of(t * tt, tt), tt)
        total = jnp.zeros((tt, LANES), jnp.float32)
        for j in range(D // LANES):
            v = x_ref[rows, j * LANES:(j + 1) * LANES].astype(jnp.float32)
            total = total + v * v
        mean = jnp.sum(total, axis=1, keepdims=True) / D
        inv_ref[rows, :] = jnp.broadcast_to(lax.rsqrt(mean + 1e-05), (tt, LANES))
        cosine = cos_ref[rows, :]
        sine = sin_ref[rows, :]
        for h in range(KVW // HEAD_DIM):
            v = cot_ref[rows, h * HEAD_DIM:(h + 1) * HEAD_DIM].astype(jnp.float32)
            pre_ref[rows, h * HEAD_DIM:(h + 1) * HEAD_DIM] = (
                v * cosine + pltpu.roll(v, HEAD_DIM // 2, 1) * sine
            ).astype(jnp.bfloat16)

    lane = lax.broadcasted_iota(jnp.int32, (BLK, LANES), 1)

    def one_owner(owner, store):
        start = pl.multiple_of(owner * tile, tile)
        inv = inv_ref[:, :1]
        normed = (
            x_ref[:, pl.ds(start, tile)].astype(jnp.float32) * inv
            * gain_ref[:, pl.ds(start, tile)]
        ).astype(jnp.bfloat16)
        for n in range(KVW // 256):
            product = lax.dot_general(
                normed, pre_ref[:, n * 256:(n + 1) * 256], (((0,), (0,)), ((), ())),
                preferred_element_type=jnp.float32,
            )
            sums[2 * n] = product[:, :LANES]
            sums[2 * n + 1] = product[:, LANES:]
        for s in range(STREAMS):
            for pair in range(rows_dp // 2):
                both = []
                for j in (2 * pair, 2 * pair + 1):
                    halves = []
                    for k in (2 * s, 2 * s + 1):
                        col = cols_ref[owner * rows_dp + j, k]
                        v = sums[col // 2, j * BLK:(j + 1) * BLK, :]
                        halves.append(pltpu.roll(v, ((col + k) % 2) * BLK, 1))
                    both.append(jnp.where(lane < BLK, halves[0], halves[1]))
                for q in range(seq):
                    v = jnp.concatenate([w[q * part:(q + 1) * part] for w in both], axis=0)
                    store(s, slot_of(plan[s], owner, q), 2 * part * pair, v)

    def exchange(s, i, size):
        axis, b = plan[s][i]
        if i == 0:
            src, dst = first.at[s], recv_first.at[s]
        else:
            begin = recv_later.shape[1] - 2 * size + 0
            src = later.at[s, pl.ds(begin, size)]
            dst = recv_later.at[s, pl.ds(begin, size)]
        return pltpu.make_async_remote_copy(
            src_ref=src, dst_ref=dst, send_sem=send_sem.at[s, i], recv_sem=recv_sem.at[s, i],
            device_id=partner(axis, b), device_id_type=pl.DeviceIdType.MESH,
        )

    mine = me_dp % 2
    half = dp * seq // 2

    @pl.loop(0, dp // 2)
    def _(o):
        def store(s, slot, row, v):
            first[s, slot, row:row + 2 * part, :] = v.astype(jnp.bfloat16)

        one_owner(2 * o + 1 - mine, store)

    copies = {}
    for s in range(STREAMS):
        copies[s, 0] = exchange(s, 0, half)
        copies[s, 0].start()

    @pl.loop(0, dp // 2)
    def _(o):
        def store(s, slot, row, v):
            acc[s, slot, row:row + 2 * part, :] = v

        one_owner(2 * o + mine, store)

    base = [0] * STREAMS
    for i in range(stages):
        size = half >> i
        for s in range(STREAMS):
            copies[s, i].wait()
            got = recv_first.at[s] if i == 0 else recv_later.at[
                s, pl.ds(recv_later.shape[1] - 2 * size, size)]
            if i == stages - 1:
                fin_ref[s] = acc[s, base[s]] + got[0].astype(jnp.float32)
                continue
            axis, b = plan[s][i + 1]
            keep = mybit(axis, b)
            h = size // 2
            give = (1 - keep) * h
            where = recv_later.shape[1] - 2 * h

            @pl.loop(0, h)
            def _(t):
                v = acc[s, base[s] + give + t] + got[give + t].astype(jnp.float32)
                later[s, where + t] = v.astype(jnp.bfloat16)

            copies[s, i + 1] = exchange(s, i + 1, h)
            copies[s, i + 1].start()

            @pl.loop(0, h)
            def _(t):
                at = base[s] + keep * h + t
                acc[s, at] = acc[s, at] + got[keep * h + t].astype(jnp.float32)

            base[s] = base[s] + keep * h


def grads_kernel(tiles, x_ref, pre_ref, inv_ref, gain_ref, blocks_ref, where_ref, out_ref,
                 held, dense, scaled, total):
    step = pl.program_id(0)
    pairs = blocks_ref.shape[0]
    width = pairs * LANES

    @pl.when(step == 0)
    def _():
        total[...] = jnp.zeros_like(total)
        held[:, MOSTR] = jnp.zeros((pairs, BLK, LANES), jnp.bfloat16)

    @pl.when(step < tiles)
    def _():
        held[:, :MOSTR] = blocks_ref[...]
        lane = lax.broadcasted_iota(jnp.int32, (BLK, LANES), 1)
        for p in range(pairs):
            row = (step * pairs + p) * 2
            for c in range(KVW // BLK):
                a = held[p, where_ref[row, c]]
                b = held[p, where_ref[row + 1, c]]
                dense[c * BLK:(c + 1) * BLK, p * LANES:(p + 1) * LANES] = jnp.where(
                    lane < BLK, a, b)
        grad = lax.dot_general(
            pre_ref[...], dense[...], (((1,), (0,)), ((), ())),
            preferred_element_type=jnp.float32,
        ) * gain_ref[...]
        scaled[step] = grad
        prod = grad * x_ref[...].astype(jnp.float32)
        part = prod[:, :LANES]
        for j in range(1, width // LANES):
            part = part + prod[:, j * LANES:(j + 1) * LANES]
        total[...] += part

    @pl.when(step == tiles - 1)
    def _():
        inv = inv_ref[:, :1]
        mean = jnp.sum(total[...], axis=1, keepdims=True) / D
        total[...] = jnp.broadcast_to(inv * inv * inv * mean, total.shape)

    @pl.when(step >= tiles)
    def _():
        inv = inv_ref[:, :1]
        back = total[:, :1]
        out_ref[...] = (
            inv * scaled[step - tiles] - back * x_ref[...].astype(jnp.float32)
        ).astype(jnp.bfloat16)


def shards(checkpoint, norm_gain, key_cotangent, positions, kept_cols, kept_count, key_blocks):
    tokens = checkpoint.shape[0]
    dp, seq = lax.axis_size("dp"), lax.axis_size("seq")
    row_blocks, col_blocks = D // BLK, KVW // BLK
    rows_dp = row_blocks // dp
    part = BLK // seq
    half = dp * seq // 2
    slab = rows_dp * part
    gain = norm_gain.reshape(1, D)

    swapped = (
        key_blocks.reshape(rows_dp // 2, 2, MOSTR, BLK, BLK)
        .transpose(0, 2, 4, 1, 3)
        .reshape(rows_dp // 2, MOSTR, BLK, LANES)
    )
    blocks = lax.all_gather(swapped, "dp", axis=0, tiled=True)

    freqs = 10000.0 ** (-2.0 * jnp.arange(HEAD_DIM // 2).astype(jnp.float32) / HEAD_DIM)
    angle = positions.astype(jnp.float32)[:, None] * freqs[None, :]
    cosine, sine = jnp.cos(angle), jnp.sin(angle)
    cosine = jnp.concatenate([cosine, cosine], axis=1)
    sine = jnp.concatenate([sine, -sine], axis=1)

    stages = bits_of(dp) + bits_of(seq)
    vmem = pl.BlockSpec(memory_space=pltpu.VMEM)
    smem = pl.BlockSpec(memory_space=pltpu.SMEM)
    pre, inv, fin = pl.pallas_call(
        functools.partial(sums_kernel, dp, seq),
        out_shape=(
            jax.ShapeDtypeStruct((tokens, KVW), jnp.bfloat16),
            jax.ShapeDtypeStruct((tokens, LANES), jnp.float32),
            jax.ShapeDtypeStruct((STREAMS, slab, LANES), jnp.float32),
        ),
        in_specs=[vmem] * 5 + [smem],
        out_specs=(vmem, vmem, vmem),
        scratch_shapes=[
            pltpu.VMEM((KVW // LANES, rows_dp * BLK, LANES), jnp.float32),
            pltpu.VMEM((STREAMS, half, slab, LANES), jnp.bfloat16),
            pltpu.VMEM((STREAMS, half, slab, LANES), jnp.float32),
            pltpu.VMEM((STREAMS, half, slab, LANES), jnp.bfloat16),
            pltpu.VMEM((STREAMS, half, slab, LANES), jnp.bfloat16),
            pltpu.VMEM((STREAMS, half, slab, LANES), jnp.bfloat16),
            pltpu.SemaphoreType.DMA((STREAMS, stages)),
            pltpu.SemaphoreType.DMA((STREAMS, stages)),
        ],
        compiler_params=pltpu.CompilerParams(
            collective_id=0, has_side_effects=True, vmem_limit_bytes=VMEM),
        cost_estimate=pl.CostEstimate(
            flops=2 * tokens * D * KVW, bytes_accessed=2 * tokens * D, transcendentals=0),
        name="sums",
    )(checkpoint, gain, key_cotangent, cosine, sine, kept_cols)

    live = lax.broadcasted_iota(jnp.int32, (row_blocks, MOSTR), 1) < kept_count[:, None]
    match = (kept_cols[:, :, None] == jnp.arange(col_blocks)[None, None, :]) & live[:, :, None]
    slot = lax.broadcasted_iota(jnp.int32, (row_blocks, MOSTR, col_blocks), 1)
    where = jnp.min(jnp.where(match, slot, MOSTR), axis=1)

    width = 512
    tiles = D // width
    pairs = width // LANES
    grads = pl.pallas_call(
        functools.partial(grads_kernel, tiles),
        grid=(2 * tiles,),
        out_shape=jax.ShapeDtypeStruct((tokens, D), jnp.bfloat16),
        in_specs=[
            pl.BlockSpec((tokens, width), lambda i: (0, i % tiles)),
            pl.BlockSpec((tokens, KVW), lambda i: (0, 0)),
            pl.BlockSpec((tokens, LANES), lambda i: (0, 0)),
            pl.BlockSpec((1, width), lambda i: (0, i % tiles)),
            pl.BlockSpec((pairs, MOSTR, BLK, LANES),
                         lambda i: (jnp.minimum(i, tiles - 1), 0, 0, 0)),
            smem,
        ],
        out_specs=pl.BlockSpec((tokens, width), lambda i: (0, jnp.maximum(i - tiles, 0))),
        scratch_shapes=[
            pltpu.VMEM((pairs, MOSTR + 1, BLK, LANES), jnp.bfloat16),
            pltpu.VMEM((KVW, width), jnp.bfloat16),
            pltpu.VMEM((tiles, tokens, width), jnp.float32),
            pltpu.VMEM((tokens, LANES), jnp.float32),
        ],
        compiler_params=pltpu.CompilerParams(vmem_limit_bytes=VMEM),
        cost_estimate=pl.CostEstimate(
            flops=2 * tokens * D * KVW, bytes_accessed=6 * tokens * D, transcendentals=0),
        name="grads",
    )(checkpoint, pre, inv, gain, blocks, where)

    mine = lax.dynamic_slice_in_dim(live, lax.axis_index("dp") * rows_dp, rows_dp, 0)
    shaped = (
        fin.reshape(STREAMS, rows_dp, part, 2, BLK)
        .transpose(1, 0, 3, 2, 4)
        .reshape(rows_dp, MOSTR, part * BLK)
    )
    divisor = math.sqrt(SEQ_LEN * dp)
    block_grad = jnp.where(mine[:, :, None], shaped / divisor, jnp.float32(0.0))
    return grads, block_grad


def solution(mesh):
    placed = (
        P(("dp", "seq"), None),
        P(),
        P(("dp", "seq"), None),
        P(("dp", "seq")),
        P(),
        P(),
        P("dp", None, None),
    )
    return jax.shard_map(
        shards,
        mesh=mesh,
        in_specs=placed,
        out_specs=(P(("dp", "seq"), None), P("dp", None, "seq")),
        check_vma=False,
    )
```

```python
import functools
import math

import jax
import jax.numpy as jnp
from jax import lax
from jax.experimental import pallas as pl
from jax.experimental.pallas import tpu as pltpu
from jax.sharding import PartitionSpec as P

D = 8192
KVW = 1024
HEAD_DIM = 128
BLK = 64
MOSTR = 6
SEQ_LEN = 1024
STREAMS = MOSTR // 2
LANES = 128
VMEM = 58 * 1024 * 1024


def bits_of(n):
    return int(math.log2(n))


def stage_plan(dp, seq):
    low = ("dp", 0)
    high = [("dp", b) for b in range(1, bits_of(dp))]
    seqs = [("seq", b) for b in range(bits_of(seq))]
    if dp == 16 and seq == 2:
        y, z1, z2 = high
        (x,) = seqs
        return [[low, x, y, z1, z2], [low, y, x, z1, z2], [low, z1, z2, x, y]]
    return [[low] + seqs + high, [low] + high + seqs, [low] + high[::-1] + seqs]


def bit(value, b):
    return (value // (1 << b)) % 2


def slot_of(order, dp_index, seq_index):
    place = 0
    for axis, b in order[1:]:
        place = place * 2 + bit(dp_index if axis == "dp" else seq_index, b)
    return place


def gather_plan(dp, seq):
    steps = [("dp", b) for b in reversed(range(bits_of(dp)))]
    if seq == 2:
        swap = steps[:-1] + [("seq", 0)] + steps[-1:]
        return [steps, swap, swap]
    return [steps] * STREAMS


def sums_kernel(dp, seq, x_ref, gain_ref, cot_ref, cos_ref, sin_ref, cols_ref, own_ref,
                pre_ref, inv_ref, fin_ref, all_ref,
                sums, first, acc, later, recv_first, recv_later, send_sem, recv_sem,
                gather_send, gather_recv, local_sem):
    tokens = x_ref.shape[0]
    rows_dp = (D // BLK) // dp
    part = BLK // seq
    tile = rows_dp * BLK
    plan = stage_plan(dp, seq)
    stages = len(plan[0])
    me_dp = lax.axis_index("dp")
    me_seq = lax.axis_index("seq")

    def partner(axis, b):
        mine = me_dp if axis == "dp" else me_seq
        other = mine + (1 << b) - 2 * (1 << b) * bit(mine, b)
        return (other, me_seq) if axis == "dp" else (me_dp, other)

    def mybit(axis, b):
        return bit(me_dp if axis == "dp" else me_seq, b)

    barrier = pltpu.get_barrier_semaphore()
    for axis, b in plan[0]:
        pl.semaphore_signal(barrier, inc=1, device_id=partner(axis, b),
                            device_id_type=pl.DeviceIdType.MESH)
    pl.semaphore_wait(barrier, stages)

    steps = gather_plan(dp, seq)

    def slots(s, i):
        split = ("seq", 0) in steps[s]
        if not split or i > steps[s].index(("seq", 0)):
            return pl.ds(2 * s, 2)
        return pl.ds(2 * s + me_seq, 1)

    def gather(s, i):
        axis, b = steps[s][i]
        n = 1 << sum(1 for a, _ in steps[s][:i] if a == "dp")
        src = own_ref if i == 0 else all_ref.at[pl.ds(0, n)]
        dst = all_ref.at[pl.ds(n, n) if axis == "dp" else pl.ds(0, n)]
        return pltpu.make_async_remote_copy(
            src_ref=src.at[:, slots(s, i)], dst_ref=dst.at[:, slots(s, i)],
            send_sem=gather_send.at[s, i], recv_sem=gather_recv.at[s, i],
            device_id=partner(axis, b), device_id_type=pl.DeviceIdType.MESH,
        )

    def keep_own(s):
        return pltpu.make_async_copy(
            own_ref.at[:, slots(s, 0)], all_ref.at[pl.ds(0, 1), slots(s, 0)], local_sem.at[s])

    def advance(s, i):
        if i >= len(steps[s]):
            return
        if i == 0:
            keep_own(s).wait()
        gather(s, i).wait()
        if i + 1 < len(steps[s]):
            gather(s, i + 1).start()

    for s in (1, 2, 0):
        gather(s, 0).start()
        keep_own(s).start()

    tt = 64

    @pl.loop(0, tokens // tt)
    def _(t):
        rows = pl.ds(pl.multiple_of(t * tt, tt), tt)
        total = jnp.zeros((tt, LANES), jnp.float32)
        for j in range(D // LANES):
            v = x_ref[rows, j * LANES:(j + 1) * LANES].astype(jnp.float32)
            total = total + v * v
        mean = jnp.sum(total, axis=1, keepdims=True) / D
        inv_ref[rows, :] = jnp.broadcast_to(lax.rsqrt(mean + 1e-05), (tt, LANES))
        cosine = cos_ref[rows, :]
        sine = sin_ref[rows, :]
        for h in range(KVW // HEAD_DIM):
            v = cot_ref[rows, h * HEAD_DIM:(h + 1) * HEAD_DIM].astype(jnp.float32)
            pre_ref[rows, h * HEAD_DIM:(h + 1) * HEAD_DIM] = (
                v * cosine + pltpu.roll(v, HEAD_DIM // 2, 1) * sine
            ).astype(jnp.bfloat16)

    advance(1, 0)
    advance(2, 0)

    lane = lax.broadcasted_iota(jnp.int32, (BLK, LANES), 1)

    def one_owner(owner, store):
        start = pl.multiple_of(owner * tile, tile)
        inv = inv_ref[:, :1]
        normed = (
            x_ref[:, pl.ds(start, tile)].astype(jnp.float32) * inv
            * gain_ref[:, pl.ds(start, tile)]
        ).astype(jnp.bfloat16)
        for n in range(KVW // 256):
            product = lax.dot_general(
                normed, pre_ref[:, n * 256:(n + 1) * 256], (((0,), (0,)), ((), ())),
                preferred_element_type=jnp.float32,
            )
            sums[2 * n] = product[:, :LANES]
            sums[2 * n + 1] = product[:, LANES:]
        for s in range(STREAMS):
            for pair in range(rows_dp // 2):
                both = []
                for j in (2 * pair, 2 * pair + 1):
                    halves = []
                    for k in (2 * s, 2 * s + 1):
                        col = cols_ref[owner * rows_dp + j, k]
                        v = sums[col // 2, j * BLK:(j + 1) * BLK, :]
                        halves.append(pltpu.roll(v, ((col + k) % 2) * BLK, 1))
                    both.append(jnp.where(lane < BLK, halves[0], halves[1]))
                for q in range(seq):
                    v = jnp.concatenate([w[q * part:(q + 1) * part] for w in both], axis=0)
                    store(s, slot_of(plan[s], owner, q), 2 * part * pair, v)

    def exchange(s, i, size):
        axis, b = plan[s][i]
        if i == 0:
            src, dst = first.at[s], recv_first.at[s]
        else:
            begin = recv_later.shape[1] - 2 * size + 0
            src = later.at[s, pl.ds(begin, size)]
            dst = recv_later.at[s, pl.ds(begin, size)]
        return pltpu.make_async_remote_copy(
            src_ref=src, dst_ref=dst, send_sem=send_sem.at[s, i], recv_sem=recv_sem.at[s, i],
            device_id=partner(axis, b), device_id_type=pl.DeviceIdType.MESH,
        )

    mine = me_dp % 2
    half = dp * seq // 2

    @pl.loop(0, dp // 2)
    def _(o):
        def store(s, slot, row, v):
            first[s, slot, row:row + 2 * part, :] = v.astype(jnp.bfloat16)

        one_owner(2 * o + 1 - mine, store)

        @pl.when(o == (dp // 2) // 8)
        def _():
            advance(0, 0)
            advance(1, 1)
            advance(2, 1)

        @pl.when(o == 4 * (dp // 2) // 8)
        def _():
            advance(0, 1)
            advance(1, 2)

        @pl.when(o == 6 * (dp // 2) // 8)
        def _():
            advance(2, 2)

    copies = {}
    for s in range(STREAMS):
        copies[s, 0] = exchange(s, 0, half)
        copies[s, 0].start()

    @pl.loop(0, dp // 2)
    def _(o):
        def store(s, slot, row, v):
            acc[s, slot, row:row + 2 * part, :] = v

        one_owner(2 * o + mine, store)

        @pl.when(o == 3 * (dp // 2) // 8)
        def _():
            advance(0, 2)
            advance(1, 3)

        @pl.when(o == 7 * (dp // 2) // 8)
        def _():
            advance(2, 3)

    done = [3, 4, 4]
    base = [0] * STREAMS
    for i in range(stages):
        size = half >> i
        for s in range(STREAMS):
            copies[s, i].wait()
            got = recv_first.at[s] if i == 0 else recv_later.at[
                s, pl.ds(recv_later.shape[1] - 2 * size, size)]
            if i == stages - 1:
                fin_ref[s] = acc[s, base[s]] + got[0].astype(jnp.float32)
                continue
            axis, b = plan[s][i + 1]
            keep = mybit(axis, b)
            h = size // 2
            give = (1 - keep) * h
            where = recv_later.shape[1] - 2 * h

            @pl.loop(0, h)
            def _(t):
                v = acc[s, base[s] + give + t] + got[give + t].astype(jnp.float32)
                later[s, where + t] = v.astype(jnp.bfloat16)

            copies[s, i + 1] = exchange(s, i + 1, h)
            copies[s, i + 1].start()

            @pl.loop(0, h)
            def _(t):
                at = base[s] + keep * h + t
                acc[s, at] = acc[s, at] + got[keep * h + t].astype(jnp.float32)

            base[s] = base[s] + keep * h
        for s in range(STREAMS):
            if i == stages - 2:
                for k in range(done[s], len(steps[s])):
                    advance(s, k)


def grads_kernel(tiles, place_ref, x_ref, pre_ref, inv_ref, gain_ref, blocks_ref, where_ref,
                 out_ref, held, dense, scaled, total):
    step = pl.program_id(0)
    pairs = blocks_ref.shape[2] // BLK
    width = pairs * LANES

    @pl.when(step == 0)
    def _():
        total[...] = jnp.zeros_like(total)
        held[MOSTR] = jnp.zeros((pairs * BLK, LANES), jnp.bfloat16)

    @pl.when(step < tiles)
    def _():
        held[:MOSTR] = blocks_ref[0]
        lane = lax.broadcasted_iota(jnp.int32, (BLK, LANES), 1)
        for p in range(pairs):
            row = (step * pairs + p) * 2
            for c in range(KVW // BLK):
                a = held[where_ref[row, c], p * BLK:(p + 1) * BLK]
                b = held[where_ref[row + 1, c], p * BLK:(p + 1) * BLK]
                dense[c * BLK:(c + 1) * BLK, p * LANES:(p + 1) * LANES] = jnp.where(
                    lane < BLK, a, b)
        grad = lax.dot_general(
            pre_ref[...], dense[...], (((1,), (0,)), ((), ())),
            preferred_element_type=jnp.float32,
        ) * gain_ref[...]
        scaled[step] = grad
        prod = grad * x_ref[...].astype(jnp.float32)
        part = prod[:, :LANES]
        for j in range(1, width // LANES):
            part = part + prod[:, j * LANES:(j + 1) * LANES]
        total[...] += part

    @pl.when(step == tiles - 1)
    def _():
        inv = inv_ref[:, :1]
        mean = jnp.sum(total[...], axis=1, keepdims=True) / D
        total[...] = jnp.broadcast_to(inv * inv * inv * mean, total.shape)

    @pl.when(step >= tiles)
    def _():
        inv = inv_ref[:, :1]
        back = total[:, :1]
        out_ref[...] = (
            inv * scaled[step - tiles] - back * x_ref[...].astype(jnp.float32)
        ).astype(jnp.bfloat16)


def shards(checkpoint, norm_gain, key_cotangent, positions, kept_cols, kept_count, key_blocks):
    tokens = checkpoint.shape[0]
    dp, seq = lax.axis_size("dp"), lax.axis_size("seq")
    row_blocks, col_blocks = D // BLK, KVW // BLK
    rows_dp = row_blocks // dp
    part = BLK // seq
    half = dp * seq // 2
    slab = rows_dp * part
    gain = norm_gain.reshape(1, D)

    swapped = (
        key_blocks.reshape(rows_dp // 2, 2, MOSTR, BLK, BLK)
        .transpose(2, 0, 4, 1, 3)
        .reshape(1, MOSTR, rows_dp // 2 * BLK, LANES)
    )

    freqs = 10000.0 ** (-2.0 * jnp.arange(HEAD_DIM // 2).astype(jnp.float32) / HEAD_DIM)
    angle = positions.astype(jnp.float32)[:, None] * freqs[None, :]
    cosine, sine = jnp.cos(angle), jnp.sin(angle)
    cosine = jnp.concatenate([cosine, cosine], axis=1)
    sine = jnp.concatenate([sine, -sine], axis=1)

    stages = bits_of(dp) + bits_of(seq)
    vmem = pl.BlockSpec(memory_space=pltpu.VMEM)
    smem = pl.BlockSpec(memory_space=pltpu.SMEM)
    anywhere = pl.BlockSpec(memory_space=pl.ANY)
    pre, inv, fin, blocks = pl.pallas_call(
        functools.partial(sums_kernel, dp, seq),
        out_shape=(
            jax.ShapeDtypeStruct((tokens, KVW), jnp.bfloat16),
            jax.ShapeDtypeStruct((tokens, LANES), jnp.float32),
            jax.ShapeDtypeStruct((STREAMS, slab, LANES), jnp.float32),
            jax.ShapeDtypeStruct((dp,) + swapped.shape[1:], jnp.bfloat16),
        ),
        in_specs=[vmem] * 5 + [smem, anywhere],
        out_specs=(vmem, vmem, vmem, anywhere),
        scratch_shapes=[
            pltpu.VMEM((KVW // LANES, rows_dp * BLK, LANES), jnp.float32),
            pltpu.VMEM((STREAMS, half, slab, LANES), jnp.bfloat16),
            pltpu.VMEM((STREAMS, half, slab, LANES), jnp.float32),
            pltpu.VMEM((STREAMS, half, slab, LANES), jnp.bfloat16),
            pltpu.VMEM((STREAMS, half, slab, LANES), jnp.bfloat16),
            pltpu.VMEM((STREAMS, half, slab, LANES), jnp.bfloat16),
            pltpu.SemaphoreType.DMA((STREAMS, stages)),
            pltpu.SemaphoreType.DMA((STREAMS, stages)),
            pltpu.SemaphoreType.DMA((STREAMS, stages)),
            pltpu.SemaphoreType.DMA((STREAMS, stages)),
            pltpu.SemaphoreType.DMA((STREAMS,)),
        ],
        compiler_params=pltpu.CompilerParams(
            collective_id=0, has_side_effects=True, vmem_limit_bytes=VMEM),
        cost_estimate=pl.CostEstimate(
            flops=2 * tokens * D * KVW, bytes_accessed=2 * tokens * D, transcendentals=0),
        name="sums",
    )(checkpoint, gain, key_cotangent, cosine, sine, kept_cols, swapped)

    live = lax.broadcasted_iota(jnp.int32, (row_blocks, MOSTR), 1) < kept_count[:, None]
    match = (kept_cols[:, :, None] == jnp.arange(col_blocks)[None, None, :]) & live[:, :, None]
    slot = lax.broadcasted_iota(jnp.int32, (row_blocks, MOSTR, col_blocks), 1)
    where = jnp.min(jnp.where(match, slot, MOSTR), axis=1)

    differs = jnp.bitwise_xor(jnp.arange(dp, dtype=jnp.int32), lax.axis_index("dp"))
    place = jnp.zeros((dp,), jnp.int32)
    for b in range(bits_of(dp)):
        place = place * 2 + bit(differs, b)

    width = rows_dp * BLK
    tiles = dp
    pairs = width // LANES
    grads = pl.pallas_call(
        functools.partial(grads_kernel, tiles),
        grid_spec=pltpu.PrefetchScalarGridSpec(
            num_scalar_prefetch=1,
            grid=(2 * tiles,),
            in_specs=[
                pl.BlockSpec((tokens, width), lambda i, place: (0, i % tiles)),
                pl.BlockSpec((tokens, KVW), lambda i, place: (0, 0)),
                pl.BlockSpec((tokens, LANES), lambda i, place: (0, 0)),
                pl.BlockSpec((1, width), lambda i, place: (0, i % tiles)),
                pl.BlockSpec((1, MOSTR, pairs * BLK, LANES),
                             lambda i, place: (place[jnp.minimum(i, tiles - 1)], 0, 0, 0)),
                smem,
            ],
            out_specs=pl.BlockSpec(
                (tokens, width), lambda i, place: (0, jnp.maximum(i - tiles, 0))),
            scratch_shapes=[
                pltpu.VMEM((MOSTR + 1, pairs * BLK, LANES), jnp.bfloat16),
                pltpu.VMEM((KVW, width), jnp.bfloat16),
                pltpu.VMEM((tiles, tokens, width), jnp.float32),
                pltpu.VMEM((tokens, LANES), jnp.float32),
            ],
        ),
        out_shape=jax.ShapeDtypeStruct((tokens, D), jnp.bfloat16),
        compiler_params=pltpu.CompilerParams(vmem_limit_bytes=VMEM),
        cost_estimate=pl.CostEstimate(
            flops=2 * tokens * D * KVW, bytes_accessed=6 * tokens * D, transcendentals=0),
        name="grads",
    )(place, checkpoint, pre, inv, gain, blocks, where)

    mine = lax.dynamic_slice_in_dim(live, lax.axis_index("dp") * rows_dp, rows_dp, 0)
    shaped = (
        fin.reshape(STREAMS, rows_dp, part, 2, BLK)
        .transpose(1, 0, 3, 2, 4)
        .reshape(rows_dp, MOSTR, part * BLK)
    )
    divisor = math.sqrt(SEQ_LEN * dp)
    block_grad = jnp.where(mine[:, :, None], shaped / divisor, jnp.float32(0.0))
    return grads, block_grad


def solution(mesh):
    placed = (
        P(("dp", "seq"), None),
        P(),
        P(("dp", "seq"), None),
        P(("dp", "seq")),
        P(),
        P(),
        P("dp", None, None),
    )
    return jax.shard_map(
        shards,
        mesh=mesh,
        in_specs=placed,
        out_specs=(P(("dp", "seq"), None), P("dp", None, "seq")),
        check_vma=False,
    )
```
